768 devices in a mesh: users: 96 (over x, z, core), items: 8 (over y).
Axes of the slice: x: 4, y: 8, z: 12, core: 2. Of those that a mesh axis runs over, the one named last changes fastest.
Arguments:
- user_factors: float32 [49152, 512], P('users'), may hold values from -6 to 6
- item_factors: bfloat16 [8, 12288, 512], P('items', 'users'), may hold values from -0.25 to 0.25
- tile_weights: bfloat16 [96, 8, 16, 128, 128], P('users', 'items'), may hold values from 0 to 4, as said below
- tile_scores: bfloat16 [96, 8, 16, 128, 128], P('users', 'items'), may hold values from -6 to 6
- tile_users: int32 [96, 8, 16], P('users', 'items'), may hold values from 0 to 3
- tile_items: int32 [96, 8, 16], P('users', 'items'), may hold values from 0 to 95
- tile_count: int32 [96, 8], P('users', 'items'), may hold values from 4 to 16, as said below
Outputs:
- new_factors: float32 [49152, 512], P('users')
The draws below stay inside these ranges and needn't reach their ends.
Inputs may be any that keep to these rules, and one draw needn't show every extreme that they name: `tile_count`: every device's list has between a quarter of 16 and 16 live slots, and one device has all 16 live in every draw. `tile_weights`: about half of the entries are zero.
All inputs are finite; a program needn't handle non-finite values.
Results may differ from the reference program's by a relative error of at most 0.00088.
The reference program's roundings to bfloat16 on the way (of `errors`) count: a program that leaves them out, or rounds other values in their place, can miss the bound.
Values may be sent and summed in bfloat16 or wider, within the bound.
No kernel may reach another device: no remote copies, remote signals or barrier semaphores. Data moves between devices by JAX's collectives and lax.ppermute only.
A program may use at most 64 MiB of HBM per device.

```python
import math
import jax
import jax.numpy as jnp
from jax import lax

D = 512
BLK = 128
SWEEP = 2
CG_STEPS = 3
UB_DEV = 4
TILE_MAX = 16
NUM_USERS = 49152
GROUP_BLOCKS = 96
NUM_ITEMS = 98304
N_USERS = 96
N_ITEMS = 8


def draw_tile_weights(key, part):
    key = jax.random.fold_in(key, 7)
    first, second = jax.random.split(key)
    shape = (N_USERS, N_ITEMS, TILE_MAX, BLK, BLK)
    observed = jax.random.bernoulli(first, 0.5, shape).astype(jnp.float32)
    level = jnp.exp(jax.random.uniform(second, shape, jnp.float32, math.log(0.25), math.log(4.0)))
    return (observed * level).astype(jnp.bfloat16)


def draw_tile_count(key, part):
    key = jax.random.fold_in(key, 11)
    first, second = jax.random.split(key)
    counts = jax.random.randint(first, (N_USERS * N_ITEMS,), TILE_MAX // 4, TILE_MAX + 1)
    chosen = jax.random.randint(second, (), 0, N_USERS * N_ITEMS)
    counts = counts.at[chosen].set(TILE_MAX)
    return counts.reshape(N_USERS, N_ITEMS).astype(jnp.int32)


def place_ends(result, rng, smallest, top_value):
    shape = result.shape
    place = [jax.random.randint(jax.random.fold_in(rng, axis), (), 0, shape[axis]) for axis in range(len(shape))]
    result = result.at[tuple(place)].set(smallest)
    longest = shape.index(max(shape))
    place[longest] = (place[longest] + 1) % shape[longest]
    return result.at[tuple(place)].set(top_value)


def block_levels(rng, shape, cuts, least, top_value):
    def one(axis_at, shards_of):
        draws = jax.random.uniform(jax.random.fold_in(jax.random.fold_in(rng, 6), axis_at), (shards_of,), jnp.float32, least / len(cuts), top_value / len(cuts))
        return jnp.repeat(jnp.exp(draws), shape[axis_at] // shards_of).reshape((-1,) + (1,) * (len(shape) - axis_at - 1))

    level = one(*cuts[0])
    for cut in cuts[1:]:
        level = level * one(*cut)
    return level


def centred(rng, dims, scale, bound, cuts=(), held_as=jnp.bfloat16):
    values = scale * jax.random.normal(rng, dims, jnp.float32)
    if cuts:
        values = values * block_levels(rng, dims, cuts, -0.22, 0.18)
    return jnp.clip(values, -bound, bound).astype(held_as)


def setup_inputs(seed: int = 0) -> dict:
    arg_keys = jax.random.split(jax.random.key(seed), 8)
    user_factors = centred(arg_keys[0], (NUM_USERS, D), 1.0, 6.0, ((0, 96),), jnp.float32)
    item_factors = centred(arg_keys[1], (N_ITEMS, GROUP_BLOCKS * BLK, D), D ** -0.5, 0.25, ((0, 8), (1, 96)))
    tile_weights = draw_tile_weights(jax.random.fold_in(arg_keys[7], 71), 0)
    tile_scores = centred(arg_keys[3], (N_USERS, N_ITEMS, TILE_MAX, BLK, BLK), 1.0, 6.0, ((0, 96), (1, 8)))
    tile_users = place_ends(jax.random.randint(arg_keys[4], (N_USERS, N_ITEMS, TILE_MAX), 0, UB_DEV), jax.random.fold_in(arg_keys[4], 1), 0, UB_DEV - 1).astype(jnp.int32)
    tile_items = place_ends(jax.random.randint(arg_keys[5], (N_USERS, N_ITEMS, TILE_MAX), 0, GROUP_BLOCKS), jax.random.fold_in(arg_keys[5], 1), 0, GROUP_BLOCKS - 1).astype(jnp.int32)
    tile_count = draw_tile_count(jax.random.fold_in(arg_keys[7], 71), 0)
    return dict(user_factors=user_factors, item_factors=item_factors, tile_weights=tile_weights, tile_scores=tile_scores, tile_users=tile_users, tile_items=tile_items, tile_count=tile_count)


implicit_scale = 8.0
ridge_weight = 1.0


def tile_terms(rows_bf, live_weights, hblocks):
    scores = jnp.einsum('gtuk,gtik->gtui', rows_bf.astype(jnp.float32), hblocks.astype(jnp.float32))
    scaled = (scores * live_weights.astype(jnp.float32)).astype(jnp.bfloat16)
    return jnp.einsum('gtui,gtik->gtuk', scaled.astype(jnp.float32), hblocks.astype(jnp.float32))


def group_sum(owners, terms):
    summed = jnp.einsum('gtb,gtuk->buk', owners, terms, precision=lax.Precision.HIGHEST)
    return summed.reshape(-1, BLK)


def reference(user_factors, item_factors, tile_weights, tile_scores, tile_users, tile_items, tile_count):
    width = SWEEP * BLK
    flat = item_factors.reshape(-1, D)
    gram = jnp.dot(flat[:, :width].T, flat, preferred_element_type=jnp.float32)
    implicit = implicit_scale * D / NUM_ITEMS
    group_slices = item_factors[:, :, :width]

    def solve_shard(inputs):
        factors, weights, scores, user_idx, item_idx, counts = inputs
        live = jnp.arange(TILE_MAX)[None, :] < counts[:, None]
        live_weights = weights * live[:, :, None, None].astype(jnp.bfloat16)
        owners = (user_idx[:, :, None] == jnp.arange(UB_DEV)[None, None, :]).astype(jnp.float32)
        predicted = scores.astype(jnp.float32)
        for block in range(SWEEP):
            low = block * BLK
            high = low + BLK
            columns = group_slices[:, :, low:high].reshape(N_ITEMS, GROUP_BLOCKS, BLK, BLK)
            hblocks = jax.vmap(lambda table, index: table[index])(columns, item_idx)
            gram_rows = gram[low:high]
            gram_diag = gram_rows[:, low:high]
            current = factors[:, low:high]
            errors = ((predicted - 1.0) * live_weights.astype(jnp.float32)).astype(jnp.bfloat16)
            error_terms = jnp.einsum('gtui,gtik->gtuk', errors.astype(jnp.float32), hblocks.astype(jnp.float32))
            local_grad = implicit * jnp.dot(factors, gram_rows.T, precision=lax.Precision.HIGHEST) + ridge_weight * current
            grad = local_grad + group_sum(owners, error_terms)
            resid = -grad
            direction = resid
            delta = jnp.zeros_like(resid)
            norm_now = jnp.sum(resid * resid, axis=1, keepdims=True)
            for step in range(CG_STEPS):
                dir_bf = direction.astype(jnp.bfloat16).reshape(UB_DEV, BLK, BLK)[user_idx]
                local_part = implicit * jnp.dot(direction, gram_diag, precision=lax.Precision.HIGHEST) + ridge_weight * direction
                image = local_part + group_sum(owners, tile_terms(dir_bf, live_weights, hblocks))
                alpha = norm_now / jnp.sum(direction * image, axis=1, keepdims=True)
                delta = delta + alpha * direction
                resid = resid - alpha * image
                if step + 1 < CG_STEPS:
                    norm_next = jnp.sum(resid * resid, axis=1, keepdims=True)
                    direction = resid + (norm_next / norm_now) * direction
                    norm_now = norm_next
            factors = factors.at[:, low:high].set(current + delta)
            if block + 1 < SWEEP:
                step_rows = delta.astype(jnp.bfloat16).reshape(UB_DEV, BLK, BLK)[user_idx]
                predicted = predicted + jnp.einsum('gtuk,gtik->gtui', step_rows.astype(jnp.float32), hblocks.astype(jnp.float32))
        return factors

    shards = lax.map(solve_shard, (user_factors.reshape(N_USERS, UB_DEV * BLK, D), tile_weights, tile_scores, tile_users, tile_items, tile_count))
    return shards.reshape(NUM_USERS, D)
```

```python
import functools

import jax
import jax.numpy as jnp
from jax import lax
from jax.experimental import pallas as pl
from jax.experimental.pallas import tpu as pltpu
from jax.sharding import Mesh
from jax.sharding import PartitionSpec as P

D = 512
BLK = 128
SWEEP = 2
CG_STEPS = 3
UB_DEV = 4

implicit_scale = 8.0
ridge_weight = 1.0

X_CHIPS = 4
CORES = 2

NT = (((1,), (1,)), ((), ()))
NN = (((1,), (0,)), ((), ()))
TN = (((0,), (0,)), ((), ()))


def spread(value, axis):
    n = lax.axis_size(axis)
    copies = jnp.broadcast_to(value[None], (n,) + value.shape)
    return lax.all_to_all(copies, axis, 0, 0)


def swap_cores(value):
    return lax.ppermute(value, "core", [(0, 1), (1, 0)])


def pick_kernel(place_ref, mine_ref, other_ref, out_ref, sems):
    tiles = place_ref.shape[0]
    per_core = mine_ref.shape[0]

    def copy(source, row, t):
        return pltpu.make_async_copy(
            source.at[row],
            out_ref.at[pl.ds((t // 2) * BLK, BLK), pl.ds((t % 2) * BLK, BLK)],
            sems.at[t],
        )

    for t in range(tiles):
        place = place_ref[t]

        @pl.when(place < per_core)
        def _():
            copy(mine_ref, place, t).start()

        @pl.when(place >= per_core)
        def _():
            copy(other_ref, place - per_core, t).start()

    for t in range(tiles):
        copy(mine_ref, 0, t).wait()


def pick(place, mine, other):
    tiles = place.shape[0]
    return pl.pallas_call(
        pick_kernel,
        out_shape=jax.ShapeDtypeStruct((tiles // 2 * BLK, 2 * BLK), jnp.bfloat16),
        in_specs=[
            pl.BlockSpec(memory_space=pltpu.SMEM),
            pl.BlockSpec(memory_space=pl.ANY),
            pl.BlockSpec(memory_space=pl.ANY),
        ],
        out_specs=pl.BlockSpec(memory_space=pltpu.VMEM),
        scratch_shapes=[pltpu.SemaphoreType.DMA((tiles,))],
        name="pick",
    )(place, mine, other)


def widen_kernel(owner_ref, pack_ref, wide_ref):
    groups = pack_ref.shape[0]
    tiles = owner_ref.shape[0] // groups

    for pair in range(tiles // 2):

        def body(group, carry):
            rows = []
            for half in range(2):
                t = 2 * pair + half
                owner = owner_ref[group * tiles + t]
                weights = pack_ref[group, t].astype(jnp.float32)
                for block in range(UB_DEV):
                    keep = (owner == block).astype(jnp.float32)
                    rows.append(weights * keep)
            column = pl.multiple_of((group * (tiles // 2) + pair) * BLK, BLK)
            wide_ref[:, pl.ds(column, BLK)] = jnp.concatenate(rows, axis=0).astype(jnp.bfloat16)
            return carry

        lax.fori_loop(0, groups, body, 0)


def widen(owner, pack):
    groups, _, own, _ = pack.shape
    rows = 2 * UB_DEV * own
    return pl.pallas_call(
        widen_kernel,
        out_shape=jax.ShapeDtypeStruct((rows, owner.shape[0] // 2 * BLK), jnp.bfloat16),
        in_specs=[
            pl.BlockSpec(memory_space=pltpu.SMEM),
            pl.BlockSpec(memory_space=pltpu.VMEM),
        ],
        out_specs=pl.BlockSpec(memory_space=pltpu.VMEM),
        name="widen",
    )(owner, pack)


def exact_dot(left, right, dims):
    return lax.dot_general(
        left, right, dims, precision=lax.Precision.HIGHEST, preferred_element_type=jnp.float32
    )


def solve_kernel(
    low, implicit, last, factors_ref, gram_ref, table_ref, wide_ref, side_ref, *rest
):
    if last:
        (out_ref,) = rest
    else:
        out_ref, errors_ref = rest
    users = factors_ref.shape[0]
    rows, columns = wide_ref.shape
    width = 1024
    chunks = columns // width
    tiles = width // BLK

    def pieces(c):
        at = pl.ds(c * width, width)
        return table_ref[at, :], wide_ref[:, at].astype(jnp.float32)

    def scores(c):
        parts = []
        for pair in range(tiles):
            halves = [side_ref[c, 2 * tiles + 2 * pair + half] for half in range(2)]
            parts.append(jnp.concatenate([h for h in halves for _ in range(UB_DEV)], axis=0))
        return jnp.concatenate(parts, axis=1).astype(jnp.float32)

    def fold(total):
        return total[:users, :BLK] + total[users:, BLK:]

    def pair_rows(value):
        value = value.astype(jnp.bfloat16)
        none = jnp.zeros_like(value)
        return jnp.concatenate(
            [jnp.concatenate([value, none], axis=1), jnp.concatenate([none, value], axis=1)], axis=0
        )

    def tile_terms(direction):
        both = pair_rows(direction)
        total = jnp.zeros((rows, 2 * BLK), jnp.float32)
        for c in range(chunks):
            table, weights = pieces(c)
            seen = lax.dot_general(both, table, NT, preferred_element_type=jnp.float32)
            scaled = (seen * weights).astype(jnp.bfloat16)
            total += lax.dot_general(scaled, table, NN, preferred_element_type=jnp.float32)
        return fold(total)

    total = jnp.zeros((rows, 2 * BLK), jnp.float32)
    for c in range(chunks):
        table, weights = pieces(c)
        if low == 0:
            errors = ((scores(c) - 1.0) * weights).astype(jnp.bfloat16)
        else:
            errors = side_ref[:, pl.ds(c * width, width)]
        total += lax.dot_general(errors, table, NN, preferred_element_type=jnp.float32)

    factors = factors_ref[...]
    current = factors[:, low : low + BLK]
    gram_rows = gram_ref[low : low + BLK, :]
    gram_diag = gram_rows[:, low : low + BLK]
    grad = implicit * exact_dot(factors, gram_rows, NT) + ridge_weight * current + fold(total)
    resid = -grad
    direction = resid
    delta = jnp.zeros_like(resid)
    norm_now = jnp.sum(resid * resid, axis=1, keepdims=True)
    for step in range(CG_STEPS):
        local_part = implicit * exact_dot(direction, gram_diag, NN) + ridge_weight * direction
        image = local_part + tile_terms(direction)
        alpha = norm_now / jnp.sum(direction * image, axis=1, keepdims=True)
        delta = delta + alpha * direction
        resid = resid - alpha * image
        if step + 1 < CG_STEPS:
            norm_next = jnp.sum(resid * resid, axis=1, keepdims=True)
            direction = resid + norm_next / norm_now * direction
            norm_now = norm_next
    if low:
        out_ref[:, :low] = factors[:, :low]
    out_ref[:, low : low + BLK] = current + delta
    if last:
        return
    out_ref[:, low + BLK :] = factors[:, low + BLK :]
    both = pair_rows(delta)
    for c in range(chunks):
        table, weights = pieces(c)
        seen = lax.dot_general(both, table, NT, preferred_element_type=jnp.float32)
        predicted = scores(c) + seen
        errors_ref[:, pl.ds(c * width, width)] = ((predicted - 1.0) * weights).astype(jnp.bfloat16)


def solve(block, implicit, factors, gram, table, wide, side):
    last = block + 1 == SWEEP
    users = factors.shape[0]
    out_width = SWEEP * BLK if last else D
    shapes = [jax.ShapeDtypeStruct((users, out_width), jnp.float32)]
    if not last:
        shapes.append(jax.ShapeDtypeStruct(wide.shape, jnp.bfloat16))
    return pl.pallas_call(
        functools.partial(solve_kernel, block * BLK, implicit, last),
        out_shape=shapes,
        in_specs=[pl.BlockSpec(memory_space=pltpu.VMEM)] * 5,
        out_specs=[pl.BlockSpec(memory_space=pltpu.VMEM)] * len(shapes),
        compiler_params=pltpu.CompilerParams(vmem_limit_bytes=40 * 1024 * 1024),
        name="solve%d" % block,
    )(factors, gram, table, wide, side)


def local(
    user_factors, item_factors, tile_weights, tile_scores, tile_users, tile_items, tile_count
):
    n_items = lax.axis_size("items")
    n_x = lax.axis_size("x")
    n_z = lax.axis_size("z")
    tiles = tile_weights.shape[2]
    own = BLK // n_items
    width = SWEEP * BLK
    total_items = item_factors.shape[1] * n_x * n_z * CORES * n_items
    implicit = implicit_scale * D / total_items
    core = lax.axis_index("core")
    group = lax.axis_index("items")
    own_items = item_factors[0]

    line = lax.all_gather(own_items, "z", axis=0)
    item_idx = tile_items[0, 0]
    chip_block = item_idx // CORES
    place = chip_block + (item_idx % CORES != core).astype(jnp.int32) * (n_x * n_z)

    def group_blocks(line_columns):
        mine = spread(line_columns, "x").reshape(n_x * n_z, BLK, BLK)
        other = swap_cores(mine)
        return lax.all_gather(pick(place, mine, other), "items", axis=0, tiled=True)

    table0 = group_blocks(spread(own_items[:, :BLK], "z"))
    table1 = group_blocks(line[:, :, BLK:width])

    live = jnp.arange(tiles) < tile_count[0, 0]
    live_weights = tile_weights[0, 0] * live[:, None, None].astype(jnp.bfloat16)
    owner_rows = jnp.broadcast_to(
        tile_users[0, 0].astype(jnp.bfloat16)[None, None, :, None], (n_items, 1, tiles, BLK)
    )
    owner_rows = jnp.pad(owner_rows, ((0, 0), (0, 0), (0, own - tiles), (0, 0)))

    def by_user(value):
        return value.reshape(tiles, n_items, own, BLK).transpose(1, 0, 2, 3)

    pack = jnp.concatenate([by_user(live_weights), by_user(tile_scores[0, 0]), owner_rows], axis=1)
    pack = lax.all_to_all(pack, "items", 0, 0)
    owner = pack[:, 2 * tiles, :tiles, 0].astype(jnp.int32).reshape(-1)
    wide = widen(owner, pack)

    line_items = line.reshape(n_z * BLK, D)
    partial = lax.dot_general(
        line_items[:, :width], line_items, TN, preferred_element_type=jnp.float32
    ).reshape(CORES, BLK, D)
    half = jnp.where(core == 0, partial[0], partial[1])
    send = jnp.where(core == 0, partial[1], partial[0])
    half = half + swap_cores(send)
    shares = half.reshape(n_x * n_items, -1, D)
    share = jnp.sum(lax.all_to_all(shares, ("x", "items"), 0, 0), axis=0)
    half = spread(share, ("x", "items")).reshape(BLK, D)
    there = swap_cores(half)
    gram = jnp.concatenate(
        [jnp.where(core == 0, half, there), jnp.where(core == 0, there, half)], axis=0
    )

    factors = lax.dynamic_index_in_dim(
        user_factors.reshape(UB_DEV, n_items, own, D), group, axis=1, keepdims=False
    ).reshape(UB_DEV * own, D)
    factors, errors = solve(0, implicit, factors, gram, table0, wide, pack)
    (swept,) = solve(1, implicit, factors, gram, table1, wide, errors)
    swept = spread(swept, "items").reshape(n_items, UB_DEV, own, width)
    swept = swept.transpose(1, 0, 2, 3).reshape(-1, width)
    return jnp.concatenate([swept, user_factors[:, width:]], axis=1)


def solution(mesh):
    n_users, n_items = mesh.devices.shape
    n_z = n_users // (X_CHIPS * CORES)
    chips = Mesh(
        mesh.devices.reshape(X_CHIPS, n_z, CORES, n_items), ("x", "z", "core", "items")
    )
    users = ("x", "z", "core")
    placed = (
        P(users, None),
        P("items", users, None),
        P(users, "items", None, None, None),
        P(users, "items", None, None, None),
        P(users, "items", None),
        P(users, "items", None),
        P(users, "items"),
    )
    return jax.shard_map(
        local, mesh=chips, in_specs=placed, out_specs=P(users, None), check_vma=False
    )
```

```python
import functools

import jax
import jax.numpy as jnp
from jax import lax
from jax.experimental import pallas as pl
from jax.experimental.pallas import tpu as pltpu
from jax.sharding import Mesh
from jax.sharding import PartitionSpec as P

D = 512
BLK = 128
SWEEP = 2
CG_STEPS = 3
UB_DEV = 4

implicit_scale = 8.0
ridge_weight = 1.0

X_CHIPS = 4
CORES = 2

NT = (((1,), (1,)), ((), ()))
NN = (((1,), (0,)), ((), ()))
TN = (((0,), (0,)), ((), ()))


def spread(value, axis):
    n = lax.axis_size(axis)
    copies = jnp.broadcast_to(value[None], (n,) + value.shape)
    return lax.all_to_all(copies, axis, 0, 0)


def swap_cores(value):
    return lax.ppermute(value, "core", [(0, 1), (1, 0)])


def pick_kernel(place_ref, mine_ref, other_ref, out_ref):
    tiles = place_ref.shape[0]
    per_core = mine_ref.shape[0]

    for t in range(tiles):
        place = place_ref[t]
        at = (pl.ds((t // 2) * BLK, BLK), pl.ds((t % 2) * BLK, BLK))

        @pl.when(place < per_core)
        def _():
            out_ref[at] = mine_ref[place]

        @pl.when(place >= per_core)
        def _():
            out_ref[at] = other_ref[place - per_core]


def pick(place, mine, other):
    tiles = place.shape[0]
    return pl.pallas_call(
        pick_kernel,
        out_shape=jax.ShapeDtypeStruct((tiles // 2 * BLK, 2 * BLK), jnp.bfloat16),
        in_specs=[
            pl.BlockSpec(memory_space=pltpu.SMEM),
            pl.BlockSpec(memory_space=pltpu.VMEM),
            pl.BlockSpec(memory_space=pltpu.VMEM),
        ],
        out_specs=pl.BlockSpec(memory_space=pltpu.VMEM),
        compiler_params=pltpu.CompilerParams(vmem_limit_bytes=16 * 1024 * 1024),
        name="pick",
    )(place, mine, other)


def widen_kernel(owner_ref, pack_ref, wide_ref):
    groups = pack_ref.shape[0]
    tiles = owner_ref.shape[0] // groups

    for pair in range(tiles // 2):

        def body(group, carry):
            rows = []
            for half in range(2):
                t = 2 * pair + half
                owner = owner_ref[group * tiles + t]
                weights = pack_ref[group, t].astype(jnp.float32)
                for block in range(UB_DEV):
                    keep = (owner == block).astype(jnp.float32)
                    rows.append(weights * keep)
            column = pl.multiple_of((group * (tiles // 2) + pair) * BLK, BLK)
            wide_ref[:, pl.ds(column, BLK)] = jnp.concatenate(rows, axis=0).astype(jnp.bfloat16)
            return carry

        lax.fori_loop(0, groups, body, 0)


def widen(owner, pack):
    groups, _, own, _ = pack.shape
    rows = 2 * UB_DEV * own
    return pl.pallas_call(
        widen_kernel,
        out_shape=jax.ShapeDtypeStruct((rows, owner.shape[0] // 2 * BLK), jnp.bfloat16),
        in_specs=[
            pl.BlockSpec(memory_space=pltpu.SMEM),
            pl.BlockSpec(memory_space=pltpu.VMEM),
        ],
        out_specs=pl.BlockSpec(memory_space=pltpu.VMEM),
        name="widen",
    )(owner, pack)


def exact_dot(left, right, dims):
    return lax.dot_general(
        left, right, dims, precision=lax.Precision.HIGHEST, preferred_element_type=jnp.float32
    )


def solve_kernel(
    low, implicit, last, factors_hbm, gram_hbm, table_hbm, wide_hbm, side_hbm, *rest
):
    if last:
        news_ref, *held = rest
    else:
        news_ref, factors_out, errors_ref, *held = rest
    factors_ref, gram_ref, table_ref, wide_ref, side_ref, flip_ref, whole_sems, sems = held
    users = factors_ref.shape[0]
    rows, columns = wide_ref.shape
    width = columns // sems.shape[1]
    chunks = columns // width
    tiles = width // BLK

    def load(part, c):
        at = pl.ds(c * width, width)
        source, target = ((table_hbm, table_ref), (side_hbm, side_ref), (wide_hbm, wide_ref))[part]
        if part == 0:
            source, target = source.at[at], target.at[at]
        elif part == 1 and low == 0:
            source, target = source.at[c], target.at[c]
        else:
            source, target = source.at[:, at], target.at[:, at]
        return pltpu.make_async_copy(source, target, sems.at[part, c])

    load_factors = pltpu.make_async_copy(factors_hbm, factors_ref, whole_sems.at[0])
    load_gram = pltpu.make_async_copy(gram_hbm, gram_ref, whole_sems.at[1])
    load_factors.start()
    load_gram.start()
    for c in range(chunks):
        for part in range(3 if low == 0 else 2):
            load(part, c).start()
    if low:
        for c in range(chunks):
            load(2, c).start()

    def pieces(c):
        at = pl.ds(c * width, width)
        return table_ref[at, :], flip_ref[:, at], wide_ref[:, at].astype(jnp.float32)

    def scores(c):
        parts = []
        for pair in range(tiles):
            halves = [side_ref[c, 2 * tiles + 2 * pair + half] for half in range(2)]
            parts.append(jnp.concatenate([h for h in halves for _ in range(UB_DEV)], axis=0))
        return jnp.concatenate(parts, axis=1).astype(jnp.float32)

    def fold(total):
        return total[:users, :BLK] + total[users:, BLK:]

    def pair_rows(value):
        value = value.astype(jnp.bfloat16)
        none = jnp.zeros_like(value)
        return jnp.concatenate(
            [jnp.concatenate([value, none], axis=1), jnp.concatenate([none, value], axis=1)], axis=0
        )

    def tile_terms(direction):
        both = pair_rows(direction)
        total = jnp.zeros((rows, 2 * BLK), jnp.float32)
        for c in range(chunks):
            table, flip, weights = pieces(c)
            seen = lax.dot_general(both, flip, NN, preferred_element_type=jnp.float32)
            scaled = (seen * weights).astype(jnp.bfloat16)
            total += lax.dot_general(scaled, table, NN, preferred_element_type=jnp.float32)
        return fold(total)

    load_factors.wait()
    load_gram.wait()
    factors = factors_ref[...]
    current = factors[:, low : low + BLK]
    gram_columns = gram_ref[...]
    gram_diag = gram_columns[low : low + BLK, :]
    local_grad = implicit * exact_dot(factors, gram_columns, NN) + ridge_weight * current

    total = jnp.zeros((rows, 2 * BLK), jnp.float32)
    for c in range(chunks):
        for part in range(3 if low == 0 else 2):
            load(part, c).wait()
        at = pl.ds(c * width, width)
        flip_ref[:, at] = table_ref[at, :].T
        if low == 0:
            table, _, weights = pieces(c)
            errors = ((scores(c) - 1.0) * weights).astype(jnp.bfloat16)
        else:
            at = pl.ds(c * width, width)
            table = table_ref[at, :]
            errors = side_ref[:, at]
        total += lax.dot_general(errors, table, NN, preferred_element_type=jnp.float32)

    if low:
        for c in range(chunks):
            load(2, c).wait()

    grad = local_grad + fold(total)
    resid = -grad
    direction = resid
    delta = jnp.zeros_like(resid)
    norm_now = jnp.sum(resid * resid, axis=1, keepdims=True)
    for step in range(CG_STEPS):
        local_part = implicit * exact_dot(direction, gram_diag, NN) + ridge_weight * direction
        image = local_part + tile_terms(direction)
        alpha = norm_now / jnp.sum(direction * image, axis=1, keepdims=True)
        delta = delta + alpha * direction
        resid = resid - alpha * image
        if step + 1 < CG_STEPS:
            norm_next = jnp.sum(resid * resid, axis=1, keepdims=True)
            direction = resid + norm_next / norm_now * direction
            norm_now = norm_next
    new = current + delta
    for copy in range(news_ref.shape[0]):
        news_ref[copy] = new
    if last:
        return
    if low:
        factors_out[:, :low] = factors[:, :low]
    factors_out[:, low : low + BLK] = new
    factors_out[:, low + BLK :] = factors[:, low + BLK :]
    both = pair_rows(delta)
    for c in range(chunks):
        table, flip, weights = pieces(c)
        seen = lax.dot_general(both, flip, NN, preferred_element_type=jnp.float32)
        predicted = scores(c) + seen
        errors_ref[:, pl.ds(c * width, width)] = ((predicted - 1.0) * weights).astype(jnp.bfloat16)


def solve(block, implicit, copies, factors, gram, table, wide, side):
    last = block + 1 == SWEEP
    users = factors.shape[0]
    shapes = [jax.ShapeDtypeStruct((copies, users, BLK), jnp.float32)]
    if not last:
        shapes.append(jax.ShapeDtypeStruct((users, D), jnp.float32))
        shapes.append(jax.ShapeDtypeStruct(wide.shape, jnp.bfloat16))
    operands = (factors, gram, table, wide, side)
    chunks = copies
    return pl.pallas_call(
        functools.partial(solve_kernel, block * BLK, implicit, last),
        out_shape=shapes,
        in_specs=[pl.BlockSpec(memory_space=pl.ANY)] * len(operands),
        out_specs=[pl.BlockSpec(memory_space=pltpu.VMEM)] * len(shapes),
        scratch_shapes=[pltpu.VMEM(value.shape, value.dtype) for value in operands]
        + [pltpu.VMEM(table.shape[::-1], table.dtype)]
        + [pltpu.SemaphoreType.DMA((2,)), pltpu.SemaphoreType.DMA((3, chunks))],
        compiler_params=pltpu.CompilerParams(vmem_limit_bytes=56 * 1024 * 1024),
        name="solve%d" % block,
    )(*operands)


def local(
    user_factors, item_factors, tile_weights, tile_scores, tile_users, tile_items, tile_count
):
    n_items = lax.axis_size("items")
    n_x = lax.axis_size("x")
    n_z = lax.axis_size("z")
    tiles = tile_weights.shape[2]
    own = BLK // n_items
    width = SWEEP * BLK
    total_items = item_factors.shape[1] * n_x * n_z * CORES * n_items
    implicit = implicit_scale * D / total_items
    core = lax.axis_index("core")
    group = lax.axis_index("items")
    own_items = item_factors[0]
    at_x = lax.axis_index("x")

    def along_x(value, shift):
        return lax.ppermute(value, "x", [(i, (i + shift) % n_x) for i in range(n_x)])

    live = jnp.arange(tiles) < tile_count[0, 0]
    live_weights = tile_weights[0, 0] * live[:, None, None].astype(jnp.bfloat16)
    owner_rows = jnp.broadcast_to(
        tile_users[0, 0].astype(jnp.bfloat16)[None, None, :, None], (n_items, 1, tiles, BLK)
    )
    owner_rows = jnp.pad(owner_rows, ((0, 0), (0, 0), (0, own - tiles), (0, 0)))

    def by_user(value):
        return value.reshape(tiles, n_items, own, BLK).transpose(1, 0, 2, 3)

    pack = jnp.concatenate([by_user(live_weights), by_user(tile_scores[0, 0]), owner_rows], axis=1)
    pack = pack.reshape(n_items, -1, BLK)

    partial = lax.dot_general(
        own_items, own_items[:, :width], TN, preferred_element_type=jnp.float32
    )
    half = jnp.where(core == 0, partial[:, :BLK], partial[:, BLK:])
    half = half + swap_cores(jnp.where(core == 0, partial[:, BLK:], partial[:, :BLK]))
    parts = half.reshape(n_x, -1, BLK)

    item_idx = tile_items[0, 0]
    chip = item_idx // CORES
    behind = (at_x - chip // n_z) % n_x
    place = behind * n_z + chip % n_z
    place = place + (item_idx % CORES != core).astype(jnp.int32) * (n_x * n_z)

    def round_x(blocks):
        middle = blocks.shape[0] // 2
        behind = along_x(blocks, 1)
        ahead = along_x(blocks, -1)
        opposite = [along_x(behind[:middle], 1), along_x(ahead[middle:], -1)]
        return jnp.concatenate([blocks, behind, *opposite, ahead], axis=0)

    line0 = spread(own_items[:, :BLK], "z")
    line0, parts, pack = lax.optimization_barrier((line0, parts, pack))
    mine0 = round_x(line0)
    pack = lax.all_to_all(pack, "items", 0, 0)
    picked0 = pick(place, mine0, swap_cores(mine0))
    picked0, pack = lax.optimization_barrier((picked0, pack))
    table0 = lax.all_gather(picked0, "items", axis=0, tiled=True)

    columns1, _, pack = lax.optimization_barrier((own_items[:, BLK:width], picked0, pack))
    line1 = spread(columns1, "z")
    parts, _ = lax.optimization_barrier((parts, picked0))
    share = lax.dynamic_index_in_dim(parts, at_x, axis=0, keepdims=False)
    for shift in range(1, n_x):
        part = lax.dynamic_index_in_dim(parts, (at_x + shift) % n_x, axis=0, keepdims=False)
        share = share + along_x(part, shift)
    line1, share = lax.optimization_barrier((line1, share))
    mine1 = round_x(line1)
    share = jnp.sum(lax.all_to_all(share.reshape(n_items, -1, BLK), "items", 0, 0), axis=0)
    mine1, share = lax.optimization_barrier((mine1, share))
    picked1 = pick(place, mine1, swap_cores(mine1))
    table1 = lax.all_gather(picked1, "items", axis=0, tiled=True)

    pack = pack.reshape(n_items, -1, own, BLK)
    owner = pack[:, 2 * tiles, :tiles, 0].astype(jnp.int32).reshape(-1)
    wide = widen(owner, pack)

    share = jnp.sum(spread(share, "z"), axis=0)
    share, wide = lax.optimization_barrier((share, wide))
    share = spread(share, "items").reshape(-1, BLK)
    gram = spread(share, ("x", "core")).reshape(n_x, CORES, -1, BLK)
    gram0 = gram[:, 0].reshape(D, BLK)
    gram1 = gram[:, 1].reshape(D, BLK)

    factors = lax.dynamic_index_in_dim(
        user_factors.reshape(UB_DEV, n_items, own, D), group, axis=1, keepdims=False
    ).reshape(UB_DEV * own, D)

    def all_users(news):
        news = lax.all_to_all(news, "items", 0, 0).reshape(n_items, UB_DEV, own, BLK)
        return news.transpose(1, 0, 2, 3).reshape(-1, BLK)

    news0, factors, errors = solve(0, implicit, n_items, factors, gram0, table0, wide, pack)
    (news1,) = solve(1, implicit, n_items, factors, gram1, table1, wide, errors)
    return jnp.concatenate(
        [all_users(news0), all_users(news1), user_factors[:, width:]], axis=1
    )


def solution(mesh):
    n_users, n_items = mesh.devices.shape
    n_z = n_users // (X_CHIPS * CORES)
    chips = Mesh(
        mesh.devices.reshape(X_CHIPS, n_z, CORES, n_items), ("x", "z", "core", "items")
    )
    users = ("x", "z", "core")
    placed = (
        P(users, None),
        P("items", users, None),
        P(users, "items", None, None, None),
        P(users, "items", None, None, None),
        P(users, "items", None),
        P(users, "items", None),
        P(users, "items"),
    )
    return jax.shard_map(
        local, mesh=chips, in_specs=placed, out_specs=P(users, None), check_vma=False
    )
```

```python
import functools

import jax
import jax.numpy as jnp
from jax import lax
from jax.experimental import pallas as pl
from jax.experimental.pallas import tpu as pltpu
from jax.sharding import Mesh
from jax.sharding import PartitionSpec as P

D = 512
BLK = 128
SWEEP = 2
CG_STEPS = 3
UB_DEV = 4

implicit_scale = 8.0
ridge_weight = 1.0

X_CHIPS = 4
CORES = 2

NT = (((1,), (1,)), ((), ()))
NN = (((1,), (0,)), ((), ()))
TN = (((0,), (0,)), ((), ()))


def spread(value, axis):
    n = lax.axis_size(axis)
    copies = jnp.broadcast_to(value[None], (n,) + value.shape)
    return lax.all_to_all(copies, axis, 0, 0)


def copy_kernel(items_ref, out_ref):
    columns = items_ref[:, :BLK]
    for copy in range(out_ref.shape[0]):
        out_ref[copy] = columns


def spread_first(items, axis):
    copies = pl.pallas_call(
        copy_kernel,
        out_shape=jax.ShapeDtypeStruct((lax.axis_size(axis), items.shape[0], BLK), items.dtype),
        in_specs=[pl.BlockSpec(memory_space=pltpu.VMEM)],
        out_specs=pl.BlockSpec(memory_space=pltpu.VMEM),
        name="copies",
    )(items)
    return lax.all_to_all(copies, axis, 0, 0)


def swap_cores(value):
    return lax.ppermute(value, "core", [(0, 1), (1, 0)])


def pick_kernel(place_ref, mine_ref, other_ref, out_ref):
    tiles = place_ref.shape[0]
    per_core = mine_ref.shape[0]

    for t in range(tiles):
        place = place_ref[t]
        at = (pl.ds((t // 2) * BLK, BLK), pl.ds((t % 2) * BLK, BLK))

        @pl.when(place < per_core)
        def _():
            out_ref[at] = mine_ref[place]

        @pl.when(place >= per_core)
        def _():
            out_ref[at] = other_ref[place - per_core]


def pick(place, mine, other):
    tiles = place.shape[0]
    return pl.pallas_call(
        pick_kernel,
        out_shape=jax.ShapeDtypeStruct((tiles // 2 * BLK, 2 * BLK), jnp.bfloat16),
        in_specs=[
            pl.BlockSpec(memory_space=pltpu.SMEM),
            pl.BlockSpec(memory_space=pltpu.VMEM),
            pl.BlockSpec(memory_space=pltpu.VMEM),
        ],
        out_specs=pl.BlockSpec(memory_space=pltpu.VMEM),
        compiler_params=pltpu.CompilerParams(vmem_limit_bytes=16 * 1024 * 1024),
        name="pick",
    )(place, mine, other)


def widen_kernel(owner_ref, pack_ref, wide_ref):
    groups = pack_ref.shape[0]
    tiles = owner_ref.shape[0] // groups

    for pair in range(tiles // 2):

        def body(group, carry):
            rows = []
            for half in range(2):
                t = 2 * pair + half
                owner = owner_ref[group * tiles + t]
                weights = pack_ref[group, t].astype(jnp.float32)
                for block in range(UB_DEV):
                    keep = (owner == block).astype(jnp.float32)
                    rows.append(weights * keep)
            column = pl.multiple_of((group * (tiles // 2) + pair) * BLK, BLK)
            wide_ref[:, pl.ds(column, BLK)] = jnp.concatenate(rows, axis=0).astype(jnp.bfloat16)
            return carry

        lax.fori_loop(0, groups, body, 0)


def widen(owner, pack):
    groups, _, own, _ = pack.shape
    rows = 2 * UB_DEV * own
    return pl.pallas_call(
        widen_kernel,
        out_shape=jax.ShapeDtypeStruct((rows, owner.shape[0] // 2 * BLK), jnp.bfloat16),
        in_specs=[
            pl.BlockSpec(memory_space=pltpu.SMEM),
            pl.BlockSpec(memory_space=pltpu.VMEM),
        ],
        out_specs=pl.BlockSpec(memory_space=pltpu.VMEM),
        name="widen",
    )(owner, pack)


def exact_dot(left, right, dims):
    return lax.dot_general(
        left, right, dims, precision=lax.Precision.HIGHEST, preferred_element_type=jnp.float32
    )


def solve_kernel(
    low, implicit, last, factors_hbm, gram_hbm, table_hbm, wide_hbm, side_hbm, *rest
):
    if last:
        news_ref, *held = rest
    else:
        news_ref, factors_out, errors_ref, *held = rest
    factors_ref, gram_ref, table_ref, wide_ref, side_ref, flip_ref, whole_sems, sems = held
    users = factors_ref.shape[0]
    rows, columns = wide_ref.shape
    width = columns // sems.shape[1]
    chunks = columns // width
    tiles = width // BLK

    def load(part, c):
        at = pl.ds(c * width, width)
        source, target = ((table_hbm, table_ref), (side_hbm, side_ref), (wide_hbm, wide_ref))[part]
        if part == 0:
            source, target = source.at[at], target.at[at]
        elif part == 1 and low == 0:
            source, target = source.at[c], target.at[c]
        else:
            source, target = source.at[:, at], target.at[:, at]
        return pltpu.make_async_copy(source, target, sems.at[part, c])

    load_factors = pltpu.make_async_copy(factors_hbm, factors_ref, whole_sems.at[0])
    load_gram = pltpu.make_async_copy(gram_hbm, gram_ref, whole_sems.at[1])
    load_factors.start()
    load_gram.start()
    for c in range(chunks):
        for part in range(3 if low == 0 else 2):
            load(part, c).start()
    if low:
        for c in range(chunks):
            load(2, c).start()

    def pieces(c):
        at = pl.ds(c * width, width)
        return table_ref[at, :], flip_ref[:, at], wide_ref[:, at].astype(jnp.float32)

    def scores(c):
        parts = []
        for pair in range(tiles):
            halves = [side_ref[c, 2 * tiles + 2 * pair + half] for half in range(2)]
            parts.append(jnp.concatenate([h for h in halves for _ in range(UB_DEV)], axis=0))
        return jnp.concatenate(parts, axis=1).astype(jnp.float32)

    def fold(total):
        return total[:users, :BLK] + total[users:, BLK:]

    def pair_rows(value):
        value = value.astype(jnp.bfloat16)
        none = jnp.zeros_like(value)
        return jnp.concatenate(
            [jnp.concatenate([value, none], axis=1), jnp.concatenate([none, value], axis=1)], axis=0
        )

    def tile_terms(direction):
        both = pair_rows(direction)
        total = jnp.zeros((rows, 2 * BLK), jnp.float32)
        for c in range(chunks):
            table, flip, weights = pieces(c)
            seen = lax.dot_general(both, flip, NN, preferred_element_type=jnp.float32)
            scaled = (seen * weights).astype(jnp.bfloat16)
            total += lax.dot_general(scaled, table, NN, preferred_element_type=jnp.float32)
        return fold(total)

    load_factors.wait()
    load_gram.wait()
    factors = factors_ref[...]
    current = factors[:, low : low + BLK]
    gram_columns = gram_ref[...]
    gram_diag = gram_columns[low : low + BLK, :]
    local_grad = implicit * exact_dot(factors, gram_columns, NN) + ridge_weight * current

    total = jnp.zeros((rows, 2 * BLK), jnp.float32)
    for c in range(chunks):
        for part in range(3 if low == 0 else 2):
            load(part, c).wait()
        at = pl.ds(c * width, width)
        flip_ref[:, at] = table_ref[at, :].T
        if low == 0:
            table, _, weights = pieces(c)
            errors = ((scores(c) - 1.0) * weights).astype(jnp.bfloat16)
        else:
            at = pl.ds(c * width, width)
            table = table_ref[at, :]
            errors = side_ref[:, at]
        total += lax.dot_general(errors, table, NN, preferred_element_type=jnp.float32)

    if low:
        for c in range(chunks):
            load(2, c).wait()

    grad = local_grad + fold(total)
    resid = -grad
    direction = resid
    delta = jnp.zeros_like(resid)
    norm_now = jnp.sum(resid * resid, axis=1, keepdims=True)
    for step in range(CG_STEPS):
        local_part = implicit * exact_dot(direction, gram_diag, NN) + ridge_weight * direction
        image = local_part + tile_terms(direction)
        alpha = norm_now / jnp.sum(direction * image, axis=1, keepdims=True)
        delta = delta + alpha * direction
        resid = resid - alpha * image
        if step + 1 < CG_STEPS:
            norm_next = jnp.sum(resid * resid, axis=1, keepdims=True)
            direction = resid + norm_next / norm_now * direction
            norm_now = norm_next
    new = current + delta
    for copy in range(news_ref.shape[0]):
        news_ref[copy] = new
    if last:
        return
    if low:
        factors_out[:, :low] = factors[:, :low]
    factors_out[:, low : low + BLK] = new
    factors_out[:, low + BLK :] = factors[:, low + BLK :]
    both = pair_rows(delta)
    for c in range(chunks):
        table, flip, weights = pieces(c)
        seen = lax.dot_general(both, flip, NN, preferred_element_type=jnp.float32)
        predicted = scores(c) + seen
        errors_ref[:, pl.ds(c * width, width)] = ((predicted - 1.0) * weights).astype(jnp.bfloat16)


def solve(block, implicit, copies, factors, gram, table, wide, side):
    last = block + 1 == SWEEP
    users = factors.shape[0]
    shapes = [jax.ShapeDtypeStruct((copies, users, BLK), jnp.float32)]
    if not last:
        shapes.append(jax.ShapeDtypeStruct((users, D), jnp.float32))
        shapes.append(jax.ShapeDtypeStruct(wide.shape, jnp.bfloat16))
    operands = (factors, gram, table, wide, side)
    chunks = copies
    return pl.pallas_call(
        functools.partial(solve_kernel, block * BLK, implicit, last),
        out_shape=shapes,
        in_specs=[pl.BlockSpec(memory_space=pl.ANY)] * len(operands),
        out_specs=[pl.BlockSpec(memory_space=pltpu.VMEM)] * len(shapes),
        scratch_shapes=[pltpu.VMEM(value.shape, value.dtype) for value in operands]
        + [pltpu.VMEM(table.shape[::-1], table.dtype)]
        + [pltpu.SemaphoreType.DMA((2,)), pltpu.SemaphoreType.DMA((3, chunks))],
        compiler_params=pltpu.CompilerParams(vmem_limit_bytes=56 * 1024 * 1024),
        name="solve%d" % block,
    )(*operands)


def local(
    user_factors, item_factors, tile_weights, tile_scores, tile_users, tile_items, tile_count
):
    n_items = lax.axis_size("items")
    n_x = lax.axis_size("x")
    n_z = lax.axis_size("z")
    tiles = tile_weights.shape[2]
    own = BLK // n_items
    width = SWEEP * BLK
    total_items = item_factors.shape[1] * n_x * n_z * CORES * n_items
    implicit = implicit_scale * D / total_items
    core = lax.axis_index("core")
    group = lax.axis_index("items")
    own_items = item_factors[0]
    at_x = lax.axis_index("x")

    def along_x(value, shift):
        return lax.ppermute(value, "x", [(i, (i + shift) % n_x) for i in range(n_x)])

    live = jnp.arange(tiles) < tile_count[0, 0]
    live_weights = tile_weights[0, 0] * live[:, None, None].astype(jnp.bfloat16)
    owner_rows = jnp.broadcast_to(
        tile_users[0, 0].astype(jnp.bfloat16)[None, None, :, None], (n_items, 1, tiles, BLK)
    )
    owner_rows = jnp.pad(owner_rows, ((0, 0), (0, 0), (0, own - tiles), (0, 0)))

    def by_user(value):
        return value.reshape(tiles, n_items, own, BLK).transpose(1, 0, 2, 3)

    pack = jnp.concatenate([by_user(live_weights), by_user(tile_scores[0, 0]), owner_rows], axis=1)
    pack = pack.reshape(n_items, -1, BLK)

    partial = lax.dot_general(
        own_items, own_items[:, :width], TN, preferred_element_type=jnp.float32
    )
    half = jnp.where(core == 0, partial[:, :BLK], partial[:, BLK:])
    half = half + swap_cores(jnp.where(core == 0, partial[:, BLK:], partial[:, :BLK]))
    parts = half.reshape(n_x, -1, BLK)

    item_idx = tile_items[0, 0]
    chip = item_idx // CORES
    behind = (at_x - chip // n_z) % n_x
    place = behind * n_z + chip % n_z
    place = place + (item_idx % CORES != core).astype(jnp.int32) * (n_x * n_z)

    def round_x(blocks):
        middle = blocks.shape[0] // 2
        behind = along_x(blocks, 1)
        ahead = along_x(blocks, -1)
        opposite = [along_x(behind[:middle], 1), along_x(ahead[middle:], -1)]
        return jnp.concatenate([blocks, behind, *opposite, ahead], axis=0)

    line0 = spread_first(own_items, "z")
    line0, parts, pack = lax.optimization_barrier((line0, parts, pack))
    mine0 = round_x(line0)
    pack = lax.all_to_all(pack, "items", 0, 0)
    picked0 = pick(place, mine0, swap_cores(mine0))
    picked0, pack = lax.optimization_barrier((picked0, pack))
    table0 = lax.all_gather(picked0, "items", axis=0, tiled=True)

    columns1, _, pack = lax.optimization_barrier((own_items[:, BLK:width], picked0, pack))
    line1 = spread(columns1, "z")
    parts, _ = lax.optimization_barrier((parts, picked0))
    share = lax.dynamic_index_in_dim(parts, at_x, axis=0, keepdims=False)
    for shift in range(1, n_x):
        part = lax.dynamic_index_in_dim(parts, (at_x + shift) % n_x, axis=0, keepdims=False)
        share = share + along_x(part, shift)
    line1, share = lax.optimization_barrier((line1, share))
    mine1 = round_x(line1)
    share = jnp.sum(lax.all_to_all(share.reshape(n_items, -1, BLK), "items", 0, 0), axis=0)
    mine1, share = lax.optimization_barrier((mine1, share))
    picked1 = pick(place, mine1, swap_cores(mine1))
    table1 = lax.all_gather(picked1, "items", axis=0, tiled=True)

    pack = pack.reshape(n_items, -1, own, BLK)
    owner = pack[:, 2 * tiles, :tiles, 0].astype(jnp.int32).reshape(-1)
    wide = widen(owner, pack)

    share = jnp.sum(spread(share, "z"), axis=0)
    share, wide = lax.optimization_barrier((share, wide))
    share = spread(share, "items").reshape(-1, BLK)
    gram = spread(share, ("x", "core")).reshape(n_x, CORES, -1, BLK)
    gram0 = gram[:, 0].reshape(D, BLK)
    gram1 = gram[:, 1].reshape(D, BLK)

    factors = lax.dynamic_index_in_dim(
        user_factors.reshape(UB_DEV, n_items, own, D), group, axis=1, keepdims=False
    ).reshape(UB_DEV * own, D)

    def all_users(news):
        news = lax.all_to_all(news, "items", 0, 0).reshape(n_items, UB_DEV, own, BLK)
        return news.transpose(1, 0, 2, 3).reshape(-1, BLK)

    news0, factors, errors = solve(0, implicit, n_items, factors, gram0, table0, wide, pack)
    (news1,) = solve(1, implicit, n_items, factors, gram1, table1, wide, errors)
    result = jnp.concatenate([all_users(news0), user_factors[:, BLK:]], axis=1)
    return lax.dynamic_update_slice(result, all_users(news1), (0, BLK))


def solution(mesh):
    n_users, n_items = mesh.devices.shape
    n_z = n_users // (X_CHIPS * CORES)
    chips = Mesh(
        mesh.devices.reshape(X_CHIPS, n_z, CORES, n_items), ("x", "z", "core", "items")
    )
    users = ("x", "z", "core")
    placed = (
        P(users, None),
        P("items", users, None),
        P(users, "items", None, None, None),
        P(users, "items", None, None, None),
        P(users, "items", None),
        P(users, "items", None),
        P(users, "items"),
    )
    return jax.shard_map(
        local, mesh=chips, in_specs=placed, out_specs=P(users, None), check_vma=False
    )
```

```python
import functools

import jax
import jax.numpy as jnp
from jax import lax
from jax.experimental import pallas as pl
from jax.experimental.pallas import tpu as pltpu
from jax.sharding import Mesh
from jax.sharding import PartitionSpec as P

D = 512
BLK = 128
SWEEP = 2
CG_STEPS = 3
UB_DEV = 4

implicit_scale = 8.0
ridge_weight = 1.0

X_CHIPS = 4
CORES = 2

NT = (((1,), (1,)), ((), ()))
NN = (((1,), (0,)), ((), ()))
TN = (((0,), (0,)), ((), ()))


def spread(value, axis):
    n = lax.axis_size(axis)
    copies = jnp.broadcast_to(value[None], (n,) + value.shape)
    return lax.all_to_all(copies, axis, 0, 0)


def copy_kernel(items_ref, out_ref):
    columns = items_ref[:, :BLK]
    for copy in range(out_ref.shape[0]):
        out_ref[copy] = columns


def spread_first(items, axis):
    copies = pl.pallas_call(
        copy_kernel,
        out_shape=jax.ShapeDtypeStruct((lax.axis_size(axis), items.shape[0], BLK), items.dtype),
        in_specs=[pl.BlockSpec(memory_space=pltpu.VMEM)],
        out_specs=pl.BlockSpec(memory_space=pltpu.VMEM),
        name="copies",
    )(items)
    return lax.all_to_all(copies, axis, 0, 0)


def swap_cores(value):
    return lax.ppermute(value, "core", [(0, 1), (1, 0)])


def pick_kernel(place_ref, mine_ref, other_ref, out_ref):
    tiles = place_ref.shape[0]
    per_core = mine_ref.shape[0]

    for t in range(tiles):
        place = place_ref[t]
        at = (pl.ds((t // 2) * BLK, BLK), pl.ds((t % 2) * BLK, BLK))

        @pl.when(place < per_core)
        def _():
            out_ref[at] = mine_ref[place]

        @pl.when(place >= per_core)
        def _():
            out_ref[at] = other_ref[place - per_core]


def pick(place, mine, other):
    tiles = place.shape[0]
    return pl.pallas_call(
        pick_kernel,
        out_shape=jax.ShapeDtypeStruct((tiles // 2 * BLK, 2 * BLK), jnp.bfloat16),
        in_specs=[
            pl.BlockSpec(memory_space=pltpu.SMEM),
            pl.BlockSpec(memory_space=pltpu.VMEM),
            pl.BlockSpec(memory_space=pltpu.VMEM),
        ],
        out_specs=pl.BlockSpec(memory_space=pltpu.VMEM),
        compiler_params=pltpu.CompilerParams(vmem_limit_bytes=16 * 1024 * 1024),
        name="pick",
    )(place, mine, other)


def widen_kernel(owner_ref, pack_ref, wide_ref):
    groups = pack_ref.shape[0]
    tiles = owner_ref.shape[0] // groups

    for pair in range(tiles // 2):

        def body(group, carry):
            rows = []
            for half in range(2):
                t = 2 * pair + half
                owner = owner_ref[group * tiles + t]
                weights = pack_ref[group, t].astype(jnp.float32)
                for block in range(UB_DEV):
                    keep = (owner == block).astype(jnp.float32)
                    rows.append(weights * keep)
            column = pl.multiple_of((group * (tiles // 2) + pair) * BLK, BLK)
            wide_ref[:, pl.ds(column, BLK)] = jnp.concatenate(rows, axis=0).astype(jnp.bfloat16)
            return carry

        lax.fori_loop(0, groups, body, 0)


def widen(owner, pack):
    groups, _, own, _ = pack.shape
    rows = 2 * UB_DEV * own
    return pl.pallas_call(
        widen_kernel,
        out_shape=jax.ShapeDtypeStruct((rows, owner.shape[0] // 2 * BLK), jnp.bfloat16),
        in_specs=[
            pl.BlockSpec(memory_space=pltpu.SMEM),
            pl.BlockSpec(memory_space=pltpu.VMEM),
        ],
        out_specs=pl.BlockSpec(memory_space=pltpu.VMEM),
        name="widen",
    )(owner, pack)


def exact_dot(left, right, dims):
    return lax.dot_general(
        left, right, dims, precision=lax.Precision.HIGHEST, preferred_element_type=jnp.float32
    )


def solve_kernel(
    low, implicit, last, factors_hbm, gram_hbm, table_hbm, wide_hbm, side_hbm, *rest
):
    if last:
        news_ref, *held = rest
    else:
        news_ref, factors_out, errors_ref, *held = rest
    factors_ref, gram_ref, table_ref, wide_ref, side_ref, flip_ref, whole_sems, sems = held
    users = factors_ref.shape[0]
    rows, columns = wide_ref.shape
    width = columns // sems.shape[1]
    chunks = columns // width
    tiles = width // BLK

    def load(part, c):
        at = pl.ds(c * width, width)
        source, target = ((table_hbm, table_ref), (side_hbm, side_ref), (wide_hbm, wide_ref))[part]
        if part == 0:
            source, target = source.at[at], target.at[at]
        elif part == 1 and low == 0:
            source, target = source.at[c], target.at[c]
        else:
            source, target = source.at[:, at], target.at[:, at]
        return pltpu.make_async_copy(source, target, sems.at[part, c])

    load_factors = pltpu.make_async_copy(factors_hbm, factors_ref, whole_sems.at[0])
    load_gram = pltpu.make_async_copy(gram_hbm, gram_ref, whole_sems.at[1])
    load_factors.start()
    load_gram.start()
    for c in range(chunks):
        for part in range(3 if low == 0 else 2):
            load(part, c).start()
    if low:
        for c in range(chunks):
            load(2, c).start()

    def pieces(c):
        at = pl.ds(c * width, width)
        return table_ref[at, :], flip_ref[:, at], wide_ref[:, at].astype(jnp.float32)

    def scores(c):
        parts = []
        for pair in range(tiles):
            halves = [side_ref[c, 2 * tiles + 2 * pair + half] for half in range(2)]
            parts.append(jnp.concatenate([h for h in halves for _ in range(UB_DEV)], axis=0))
        return jnp.concatenate(parts, axis=1).astype(jnp.float32)

    def fold(total):
        return total[:users, :BLK] + total[users:, BLK:]

    def pair_rows(value):
        value = value.astype(jnp.bfloat16)
        none = jnp.zeros_like(value)
        return jnp.concatenate(
            [jnp.concatenate([value, none], axis=1), jnp.concatenate([none, value], axis=1)], axis=0
        )

    def tile_terms(direction, step):
        both = pair_rows(direction)
        total = jnp.zeros((rows, 2 * BLK), jnp.float32)
        for c in range(chunks):
            if low and step == 0:
                load(2, c).wait()
            table, flip, weights = pieces(c)
            seen = lax.dot_general(both, flip, NN, preferred_element_type=jnp.float32)
            scaled = (seen * weights).astype(jnp.bfloat16)
            total += lax.dot_general(scaled, table, NN, preferred_element_type=jnp.float32)
        return fold(total)

    load_factors.wait()
    load_gram.wait()
    factors = factors_ref[...]
    current = factors[:, low : low + BLK]
    gram_columns = gram_ref[...]
    gram_diag = gram_columns[low : low + BLK, :]
    local_grad = implicit * exact_dot(factors, gram_columns, NN) + ridge_weight * current

    total = jnp.zeros((rows, 2 * BLK), jnp.float32)
    for c in range(chunks):
        for part in range(3 if low == 0 else 2):
            load(part, c).wait()
        at = pl.ds(c * width, width)
        flip_ref[:, at] = table_ref[at, :].T
        if low == 0:
            table, _, weights = pieces(c)
            errors = ((scores(c) - 1.0) * weights).astype(jnp.bfloat16)
        else:
            at = pl.ds(c * width, width)
            table = table_ref[at, :]
            errors = side_ref[:, at]
        total += lax.dot_general(errors, table, NN, preferred_element_type=jnp.float32)

    grad = local_grad + fold(total)
    resid = -grad
    direction = resid
    delta = jnp.zeros_like(resid)
    norm_now = jnp.sum(resid * resid, axis=1, keepdims=True)
    for step in range(CG_STEPS):
        local_part = implicit * exact_dot(direction, gram_diag, NN) + ridge_weight * direction
        image = local_part + tile_terms(direction, step)
        alpha = norm_now / jnp.sum(direction * image, axis=1, keepdims=True)
        delta = delta + alpha * direction
        resid = resid - alpha * image
        if step + 1 < CG_STEPS:
            norm_next = jnp.sum(resid * resid, axis=1, keepdims=True)
            direction = resid + norm_next / norm_now * direction
            norm_now = norm_next
    new = current + delta
    for copy in range(news_ref.shape[0]):
        news_ref[copy] = new
    if last:
        return
    if low:
        factors_out[:, :low] = factors[:, :low]
    factors_out[:, low : low + BLK] = new
    factors_out[:, low + BLK :] = factors[:, low + BLK :]
    both = pair_rows(delta)
    for c in range(chunks):
        table, flip, weights = pieces(c)
        seen = lax.dot_general(both, flip, NN, preferred_element_type=jnp.float32)
        predicted = scores(c) + seen
        errors_ref[:, pl.ds(c * width, width)] = ((predicted - 1.0) * weights).astype(jnp.bfloat16)


def solve(block, implicit, copies, factors, gram, table, wide, side):
    last = block + 1 == SWEEP
    users = factors.shape[0]
    shapes = [jax.ShapeDtypeStruct((copies, users, BLK), jnp.float32)]
    if not last:
        shapes.append(jax.ShapeDtypeStruct((users, D), jnp.float32))
        shapes.append(jax.ShapeDtypeStruct(wide.shape, jnp.bfloat16))
    operands = (factors, gram, table, wide, side)
    chunks = copies
    return pl.pallas_call(
        functools.partial(solve_kernel, block * BLK, implicit, last),
        out_shape=shapes,
        in_specs=[pl.BlockSpec(memory_space=pl.ANY)] * len(operands),
        out_specs=[pl.BlockSpec(memory_space=pltpu.VMEM)] * len(shapes),
        scratch_shapes=[pltpu.VMEM(value.shape, value.dtype) for value in operands]
        + [pltpu.VMEM(table.shape[::-1], table.dtype)]
        + [pltpu.SemaphoreType.DMA((2,)), pltpu.SemaphoreType.DMA((3, chunks))],
        compiler_params=pltpu.CompilerParams(vmem_limit_bytes=56 * 1024 * 1024),
        name="solve%d" % block,
    )(*operands)


def local(
    user_factors, item_factors, tile_weights, tile_scores, tile_users, tile_items, tile_count
):
    n_items = lax.axis_size("items")
    n_x = lax.axis_size("x")
    n_z = lax.axis_size("z")
    tiles = tile_weights.shape[2]
    own = BLK // n_items
    width = SWEEP * BLK
    total_items = item_factors.shape[1] * n_x * n_z * CORES * n_items
    implicit = implicit_scale * D / total_items
    core = lax.axis_index("core")
    group = lax.axis_index("items")
    own_items = item_factors[0]
    at_x = lax.axis_index("x")

    def along_x(value, shift):
        return lax.ppermute(value, "x", [(i, (i + shift) % n_x) for i in range(n_x)])

    live = jnp.arange(tiles) < tile_count[0, 0]
    live_weights = tile_weights[0, 0] * live[:, None, None].astype(jnp.bfloat16)
    owner_rows = jnp.broadcast_to(
        tile_users[0, 0].astype(jnp.bfloat16)[None, None, :, None], (n_items, 1, tiles, BLK)
    )
    owner_rows = jnp.pad(owner_rows, ((0, 0), (0, 0), (0, own - tiles), (0, 0)))

    def by_user(value):
        return value.reshape(tiles, n_items, own, BLK).transpose(1, 0, 2, 3)

    pack = jnp.concatenate([by_user(live_weights), by_user(tile_scores[0, 0]), owner_rows], axis=1)
    pack = pack.reshape(n_items, -1, BLK)

    partial = lax.dot_general(
        own_items, own_items[:, :width], TN, preferred_element_type=jnp.float32
    )
    half = jnp.where(core == 0, partial[:, :BLK], partial[:, BLK:])
    half = half + swap_cores(jnp.where(core == 0, partial[:, BLK:], partial[:, :BLK]))
    parts = half.reshape(n_x, -1, BLK)

    item_idx = tile_items[0, 0]
    chip = item_idx // CORES
    behind = (at_x - chip // n_z) % n_x
    place = behind * n_z + chip % n_z
    place = place + (item_idx % CORES != core).astype(jnp.int32) * (n_x * n_z)

    def round_x(blocks):
        middle = blocks.shape[0] // 2
        behind = along_x(blocks, 1)
        ahead = along_x(blocks, -1)
        opposite = [along_x(behind[:middle], 1), along_x(ahead[middle:], -1)]
        return jnp.concatenate([blocks, behind, *opposite, ahead], axis=0)

    line0 = spread_first(own_items, "z")
    line0, parts, pack = lax.optimization_barrier((line0, parts, pack))
    mine0 = round_x(line0)
    pack = lax.all_to_all(pack, "items", 0, 0)
    picked0 = pick(place, mine0, swap_cores(mine0))
    picked0, pack = lax.optimization_barrier((picked0, pack))
    table0 = lax.all_gather(picked0, "items", axis=0, tiled=True)

    columns1, _, pack = lax.optimization_barrier((own_items[:, BLK:width], picked0, pack))
    line1 = spread(columns1, "z")
    parts, _ = lax.optimization_barrier((parts, picked0))
    share = lax.dynamic_index_in_dim(parts, at_x, axis=0, keepdims=False)
    for shift in range(1, n_x):
        part = lax.dynamic_index_in_dim(parts, (at_x + shift) % n_x, axis=0, keepdims=False)
        share = share + along_x(part, shift)
    line1, share = lax.optimization_barrier((line1, share))
    mine1 = round_x(line1)
    share = jnp.sum(lax.all_to_all(share.reshape(n_items, -1, BLK), "items", 0, 0), axis=0)
    mine1, share = lax.optimization_barrier((mine1, share))
    picked1 = pick(place, mine1, swap_cores(mine1))
    table1 = lax.all_gather(picked1, "items", axis=0, tiled=True)

    pack = pack.reshape(n_items, -1, own, BLK)
    owner = pack[:, 2 * tiles, :tiles, 0].astype(jnp.int32).reshape(-1)
    wide = widen(owner, pack)

    share = jnp.sum(spread(share, "z"), axis=0)
    share, wide = lax.optimization_barrier((share, wide))
    share = spread(share, "items").reshape(-1, BLK)
    gram = spread(share, ("x", "core")).reshape(n_x, CORES, -1, BLK)
    gram0 = gram[:, 0].reshape(D, BLK)
    gram1 = gram[:, 1].reshape(D, BLK)

    factors = lax.dynamic_index_in_dim(
        user_factors.reshape(UB_DEV, n_items, own, D), group, axis=1, keepdims=False
    ).reshape(UB_DEV * own, D)

    def all_users(news):
        news = lax.all_to_all(news, "items", 0, 0).reshape(n_items, UB_DEV, own, BLK)
        return news.transpose(1, 0, 2, 3).reshape(-1, BLK)

    news0, factors, errors = solve(0, implicit, n_items, factors, gram0, table0, wide, pack)
    (news1,) = solve(1, implicit, n_items, factors, gram1, table1, wide, errors)
    result = jnp.concatenate([all_users(news0), user_factors[:, BLK:]], axis=1)
    return lax.dynamic_update_slice(result, all_users(news1), (0, BLK))


def solution(mesh):
    n_users, n_items = mesh.devices.shape
    n_z = n_users // (X_CHIPS * CORES)
    chips = Mesh(
        mesh.devices.reshape(X_CHIPS, n_z, CORES, n_items), ("x", "z", "core", "items")
    )
    users = ("x", "z", "core")
    placed = (
        P(users, None),
        P("items", users, None),
        P(users, "items", None, None, None),
        P(users, "items", None, None, None),
        P(users, "items", None),
        P(users, "items", None),
        P(users, "items"),
    )
    return jax.shard_map(
        local, mesh=chips, in_specs=placed, out_specs=P(users, None), check_vma=False
    )
```
